512 devices in a mesh: aux: 8 (over x, core), ao: 64 (over y, z).
Axes of the slice: x: 4, y: 8, z: 8, core: 2. Of those that a mesh axis runs over, the one named last changes fastest.
Arguments:
- tiles: bfloat16 [64, 768, 4096], P('aux', 'ao'), may hold values from -6 to 6
- slot_row_block: int32 [8, 768], P('aux', 'ao'), may hold values from 0 to 9
- tile_col: int32 [8, 768], P('aux', 'ao'), may hold values from -1 to 29, as said below
- coeff: bfloat16 [40960, 64], P('ao'), may hold values from -0.1875 to 0.1875
Outputs:
- relaid: bfloat16 [4096, 40960], P(('aux', 'ao'))
- pair_ints: float32 [4096, 64], P(('aux', 'ao'))
The draws below stay inside these ranges and needn't reach their ends.
Inputs may be any that keep to these rules, and one draw needn't show every extreme that they name: `tile_col`: in the slots p * 768 // 64 .. of one device (aux index a, ao index p) the live ones come first and number between 5 and 12; in every draw some device has all 12 slots live. Empty slots hold -1. A live value c names AO column block 10 * (p - 1) + c, which lies inside the grid of 40960 functions.
All inputs are finite; a program needn't handle non-finite values.
Results may differ from the reference program's by a relative error of at most 0.007.
Values may be sent and summed in bfloat16 or wider, within the bound.
A program may use at most 64 MiB of HBM per device.

```python
import jax
import jax.numpy as jnp
from jax import lax

SCREEN_BLOCK = 64
OCC = 64
ORBITAL_BLOCKS = 10
QD = 8
NT = 12
NAO = 40960
AUX_TOTAL = 64
SLOT_COUNT = 768
MIN_LIVE_SLOTS = 5
N_AUX = 8
N_AO = 64


def draw_tile_col(key, part):
    key = jax.random.fold_in(key, 11)
    count_key, full_key, column_key = jax.random.split(key, 3)
    devices_all = N_AUX * N_AO
    fewest = MIN_LIVE_SLOTS
    device_numbers = jnp.arange(devices_all, dtype=jnp.int32)
    live_counts = jax.random.randint(count_key, (devices_all,), fewest, NT + 1)
    full_device = jax.random.randint(full_key, (), 0, devices_all)
    live_counts = jnp.where(device_numbers == full_device, NT, live_counts)
    live_counts = jnp.where(device_numbers == (full_device + 1) % devices_all, fewest, live_counts)
    ao_place = device_numbers % N_AO
    lowest = jnp.where(ao_place == 0, ORBITAL_BLOCKS, 0)
    highest = jnp.where(ao_place == N_AO - 1, 2 * ORBITAL_BLOCKS, 3 * ORBITAL_BLOCKS)
    columns = jax.random.randint(column_key, (devices_all, NT), lowest[:, None], highest[:, None])
    slot_index = jnp.arange(NT, dtype=jnp.int32)[None, :]
    columns = jnp.where(slot_index == 0, highest[:, None] - 1, columns)
    columns = jnp.where(slot_index == 1, lowest[:, None], columns)
    columns = jnp.where(slot_index < live_counts[:, None], columns, -1)
    return columns.reshape(N_AUX, N_AO * NT).astype(jnp.int32)


def plant(drawn, own_key, least, high):
    shape = drawn.shape
    spot = [jax.random.randint(jax.random.fold_in(own_key, axis), (), 0, shape[axis]) for axis in range(len(shape))]
    drawn = drawn.at[tuple(spot)].set(least)
    longest = shape.index(max(shape))
    spot[longest] = (spot[longest] + 1) % shape[longest]
    return drawn.at[tuple(spot)].set(high)


def block_scale(stream_key, extent, shards, smallest, largest):
    def one(position, parts):
        heights = jax.random.uniform(jax.random.fold_in(jax.random.fold_in(stream_key, 6), position), (parts,), jnp.float32, smallest / len(shards), largest / len(shards))
        return jnp.repeat(jnp.exp(heights), extent[position] // parts).reshape((-1,) + (1,) * (len(extent) - position - 1))

    level = one(*shards[0])
    for cut in shards[1:]:
        level = level * one(*cut)
    return level


def normal_values(key, shape, deviation, limit, shards=(), held_as=jnp.bfloat16):
    values = jax.random.normal(key, shape, jnp.float32) * deviation
    if len(shards) > 0:
        values = block_scale(key, shape, shards, -0.22, 0.18) * values
    return jnp.clip(values, min=-limit, max=limit).astype(held_as)


def setup_inputs(seed: int = 0) -> dict:
    key_of = jax.random.split(jax.random.key(seed), 5)
    tiles = normal_values(key_of[0], (AUX_TOTAL, SLOT_COUNT, SCREEN_BLOCK * SCREEN_BLOCK), 1.0, 6.0, ((0, 8), (1, 64)))
    slot_row_block = plant(jax.random.randint(key_of[1], (N_AUX, SLOT_COUNT), 0, ORBITAL_BLOCKS), jax.random.fold_in(key_of[1], 1), 0, ORBITAL_BLOCKS - 1).astype(jnp.int32)
    tile_col = draw_tile_col(jax.random.fold_in(key_of[4], 71), 0)
    coeff = normal_values(key_of[3], (NAO, OCC), 1024 ** -0.5, 0.1875, ((0, 64),))
    return {"tiles": tiles, "slot_row_block": slot_row_block, "tile_col": tile_col, "coeff": coeff}


def band_terms(tile_block, rows, columns, coeff_block):
    slots = rows.shape[0]
    blocks = coeff_block.reshape(ORBITAL_BLOCKS, SCREEN_BLOCK, OCC)
    picked = jnp.take(blocks, rows, axis=0).astype(jnp.float32)
    quads = tile_block.reshape(tile_block.shape[0], slots, SCREEN_BLOCK, SCREEN_BLOCK).astype(jnp.float32)
    half = jnp.einsum('tmi,qtmn->tqin', picked, quads, precision=lax.Precision.HIGHEST)
    placing = (columns[:, None] == jnp.arange(3 * ORBITAL_BLOCKS, dtype=jnp.int32)[None, :]).astype(jnp.float32)
    return jnp.einsum('tc,tqin->qicn', placing, half, precision=lax.Precision.HIGHEST)


def reference(tiles, slot_row_block, tile_col, coeff):
    width = ORBITAL_BLOCKS * SCREEN_BLOCK
    total_rows = QD * OCC
    relaid_parts = []
    pair_parts = []
    for block in range(N_AUX):
        aux_tiles = tiles[block * QD:(block + 1) * QD]
        row_list = slot_row_block[block]
        col_list = tile_col[block]

        def one_device(index, whole):
            index = jnp.asarray(index).astype(jnp.int32)
            first = (index * NT).astype(jnp.int32)
            part_tiles = lax.dynamic_slice_in_dim(aux_tiles, first, NT, 1)
            part_rows = lax.dynamic_slice_in_dim(row_list, first, NT, 0)
            part_cols = lax.dynamic_slice_in_dim(col_list, first, NT, 0)
            part_coeff = lax.dynamic_slice_in_dim(coeff, (index * width).astype(jnp.int32), width, 0)
            band = band_terms(part_tiles, part_rows, part_cols, part_coeff).reshape(total_rows, 3 * width)
            start = (index * width).astype(jnp.int32)
            current = lax.dynamic_slice_in_dim(whole, start, 3 * width, 1)
            return lax.dynamic_update_slice_in_dim(whole, current + band, start, 1)

        whole = lax.fori_loop(0, N_AO, one_device, jnp.zeros((total_rows, NAO + 2 * width), jnp.float32))
        dense = whole[:, width:width + NAO].astype(jnp.bfloat16)
        relaid_parts.append(dense)
        pair_parts.append(jnp.dot(dense, coeff, preferred_element_type=jnp.float32))
    return jnp.concatenate(relaid_parts, axis=0), jnp.concatenate(pair_parts, axis=0)
```

```python
import jax
import jax.numpy as jnp
from jax import lax
from jax.experimental import pallas as pl
from jax.experimental.pallas import tpu as pltpu
from jax.sharding import PartitionSpec as P

SB = 64
OCC = 64
NB = 10
NT = 12
QD = 8
SIDE = 8
NAO = SIDE * SIDE
LANES = 128
GROUPS = 8
MESH = pl.DeviceIdType.MESH


def lower_half(shape):
    return lax.broadcasted_iota(jnp.int32, shape, len(shape) - 1) < SB


def swap_halves(x):
    return pltpu.roll(x, SB, axis=x.ndim - 1)


def doubled_blocks(coeff_ref, out_ref, first):
    for pair in range(NB // 2):
        x = coeff_ref[:, pair * LANES : (pair + 1) * LANES].astype(jnp.float32)
        y = swap_halves(x)
        low = lower_half(x.shape)
        out_ref[first + 2 * pair] = jnp.where(low, x, y).astype(jnp.bfloat16)
        out_ref[first + 2 * pair + 1] = jnp.where(low, y, x).astype(jnp.bfloat16)


def exchange_kernel(
    rows, cols, tiles, coeff, got, pair_got,
    raw, turned, send, halves, blocks, near, part, part_got, mid,
    load_sems, near_send, near_recv, main_send, main_recv, col_send, col_recv, row_send, row_recv, own_sems,
):
    aux, me = lax.axis_index("aux"), lax.axis_index("ao")
    y, z = me // SIDE, me % SIDE

    def partner(k):
        return ((y + k // SIDE) % SIDE) * SIDE + (z + k % SIDE) % SIDE

    barrier = pltpu.get_barrier_semaphore()

    @pl.loop(1, NAO)
    def _(k):
        pl.semaphore_signal(barrier, inc=1, device_id=(aux, partner(k)), device_id_type=MESH)

    loads = [pltpu.make_async_copy(tiles.at[pl.ds(4 * g, 4)], raw.at[pl.ds(4 * g, 4)], load_sems.at[g]) for g in range(3)]
    for load in loads:
        load.start()
    doubled_blocks(coeff, blocks, NB)

    for g in range(3):
        loads[g].wait()
        for sub in range(2):
            first = 4 * g + 2 * sub
            for side in range(2):
                for k in range(SB // 2):
                    v = raw[first + side, :, k * LANES : (k + 1) * LANES].astype(jnp.float32)
                    w = swap_halves(v)
                    turned[side, pl.ds(16 * k, 8), :] = v if side == 0 else w
                    turned[side, pl.ds(16 * k + 8, 8), :] = w if side == 0 else v
            left = []
            for side in range(2):
                t = first + side
                c = blocks[NB + rows[0, t]]
                left.append(jnp.where(cols[0, t] >= 0, c, jnp.zeros_like(c)))
            left = jnp.where(lower_half(left[0].shape), left[0], left[1])
            low = lower_half((SB, LANES))
            right = []
            for q in range(QD):
                a = turned[0, pl.ds(q, SB, stride=QD), :]
                b = turned[1, pl.ds(q, SB, stride=QD), :]
                right.append(jnp.concatenate([jnp.where(low, a, 0.0), jnp.where(low, 0.0, b)], axis=0).astype(jnp.bfloat16))
            half = jnp.dot(left, jnp.concatenate(right, axis=1), preferred_element_type=jnp.float32).astype(jnp.bfloat16)
            for q in range(QD):
                hq = half[:, q * LANES : (q + 1) * LANES]
                halves[2 * g + sub, pl.ds(q * OCC, OCC), :] = hq
                send[pl.ds(QD * q, QD), g, pl.ds(8 * sub, 8), :] = hq.reshape(SIDE, 8, LANES)

    pl.semaphore_wait(barrier, NAO - 1)

    near_copies = []
    for way, shift in ((0, 1), (1, NAO - 1)):
        near_copies.append(
            pltpu.make_async_remote_copy(
                coeff, near.at[way], near_send.at[way], near_recv.at[way],
                device_id=(aux, (me + shift) % NAO), device_id_type=MESH,
            )
        )
    for copy in near_copies:
        copy.start()

    own = pltpu.make_async_copy(send.at[me], got.at[me], own_sems.at[0])
    own.start()

    def ship(k):
        to = partner(k)
        pltpu.make_async_remote_copy(
            send.at[to], got.at[me], main_send, main_recv, device_id=(aux, to), device_id_type=MESH
        ).start()

    pl.loop(1, NAO // 4)(ship)

    for copy in near_copies:
        copy.wait()
    doubled_blocks(near.at[0], blocks, 0)
    doubled_blocks(near.at[1], blocks, 2 * NB)
    total = jnp.zeros((QD * OCC, LANES), jnp.float32)
    for s in range(NT // 2):
        w0 = blocks[jnp.maximum(cols[0, 2 * s], 0)]
        w1 = blocks[jnp.maximum(cols[0, 2 * s + 1], 0)]
        w = jnp.where(lower_half(w0.shape), w0, w1)
        total += lax.dot_general(
            halves[s], jnp.concatenate([w, w], axis=0), (((1,), (1,)), ((), ())), preferred_element_type=jnp.float32
        )
    high = total.astype(jnp.bfloat16)
    rest = (total - high.astype(jnp.float32)).astype(jnp.bfloat16)
    part[...] = jnp.where(lower_half(high.shape), high, rest).reshape(QD, OCC, LANES)

    own_part = pltpu.make_async_copy(part.at[y], part_got.at[y], own_sems.at[1])
    own_part.start()

    @pl.loop(1, SIDE)
    def _(k):
        to = (y + k) % SIDE
        pltpu.make_async_remote_copy(
            part.at[to], part_got.at[y], col_send, col_recv, device_id=(aux, to * SIDE + z), device_id_type=MESH
        ).start()

    pl.loop(NAO // 4, NAO)(ship)

    seven = pl.ds(0, SIDE - 1)
    own_part.wait()
    pltpu.make_async_copy(part_got.at[seven], part_got.at[seven], col_recv).wait()
    summed = part_got[0].astype(jnp.float32)
    for k in range(1, SIDE):
        summed += part_got[k].astype(jnp.float32)
    summed += swap_halves(summed)
    mid[...] = summed.reshape(SIDE, 8, LANES)
    own_mid = pltpu.make_async_copy(mid.at[z], pair_got.at[z], own_sems.at[2])
    own_mid.start()

    @pl.loop(1, SIDE)
    def _(k):
        to = (z + k) % SIDE
        pltpu.make_async_remote_copy(
            mid.at[to], pair_got.at[z], row_send, row_recv, device_id=(aux, y * SIDE + to), device_id_type=MESH
        ).start()

    own.wait()
    own_mid.wait()
    most = pl.ds(0, NAO - 1)
    pltpu.make_async_copy(part.at[seven], part.at[seven], col_send).wait()
    pltpu.make_async_copy(mid.at[seven], mid.at[seven], row_send).wait()
    pltpu.make_async_copy(send.at[most], send.at[most], main_send).wait()
    pltpu.make_async_copy(pair_got.at[seven], pair_got.at[seven], row_recv).wait()
    pltpu.make_async_copy(got.at[most], got.at[most], main_recv).wait()


def exchange(rows, cols, tiles, coeff):
    vmem, smem = pl.BlockSpec(memory_space=pltpu.VMEM), pl.BlockSpec(memory_space=pltpu.SMEM)
    dma = pltpu.SemaphoreType.DMA
    bf16, f32 = jnp.bfloat16, jnp.float32
    return pl.pallas_call(
        exchange_kernel,
        out_shape=(
            jax.ShapeDtypeStruct((NAO, 3, 16, LANES), bf16),
            jax.ShapeDtypeStruct((SIDE, 8, LANES), f32),
        ),
        in_specs=[smem, smem, pl.BlockSpec(memory_space=pl.ANY), vmem],
        out_specs=(vmem, vmem),
        scratch_shapes=[
            pltpu.VMEM((NT, QD, SB * SB), bf16),
            pltpu.VMEM((2, SB * QD, LANES), f32),
            pltpu.VMEM((NAO, 3, 16, LANES), bf16),
            pltpu.VMEM((NT // 2, QD * OCC, LANES), bf16),
            pltpu.VMEM((3 * NB, OCC, LANES), bf16),
            pltpu.VMEM((2, OCC, NB * SB), bf16),
            pltpu.VMEM((QD, OCC, LANES), bf16),
            pltpu.VMEM((SIDE, OCC, LANES), bf16),
            pltpu.VMEM((SIDE, 8, LANES), f32),
            dma((3,)), dma((2,)), dma((2,)), dma, dma, dma, dma, dma, dma, dma((3,)),
        ],
        compiler_params=pltpu.CompilerParams(collective_id=0, has_side_effects=True, vmem_limit_bytes=40 << 20),
        cost_estimate=pl.CostEstimate(flops=200_000_000, bytes_accessed=3_000_000, transcendentals=0),
        name="half_transform_exchange",
    )(rows, cols, tiles, coeff)


def place_kernel(cols, got, pair_got, relaid, pair_ints, *sums):
    per = NAO // GROUPS
    tiles_per = NB // 2
    zero = jnp.zeros((8, LANES), jnp.float32)
    for total in sums:
        total[...] = jnp.zeros(total.shape, jnp.float32)
    half_of = lax.broadcasted_iota(jnp.int32, (8, LANES), 1) // SB
    low = half_of == 0

    @pl.loop(0, per)
    def _(k):
        for s in range(NT // 2):
            for g in range(GROUPS):
                p = g * per + k
                v = got[p, s // 2, pl.ds(8 * (s % 2), 8), :].astype(jnp.float32)
                w = swap_halves(v)
                for side in range(2):
                    both = jnp.where(low, v, w) if side == 0 else jnp.where(low, w, v)
                    c = jnp.maximum(cols[0, p * NT + 2 * s + side], 0)
                    at = tiles_per * k + c // 2
                    sums[g][at] += jnp.where(half_of == c % 2, both, zero)

    for tile in range(NAO * tiles_per):
        g, local = divmod(tile, per * tiles_per)
        value = sums[g][local + tiles_per]
        if local < tiles_per and g > 0:
            value += sums[g - 1][local + (per + 1) * tiles_per]
        if local >= (per - 1) * tiles_per and g < GROUPS - 1:
            value += sums[g + 1][local - (per - 1) * tiles_per]
        relaid[:, tile * LANES : (tile + 1) * LANES] = value.astype(jnp.bfloat16)

    total = pair_got[0]
    for k in range(1, SIDE):
        total += pair_got[k]
    pair_ints[...] = total[:, :OCC]


def place(cols, got, pair_got):
    vmem, smem = pl.BlockSpec(memory_space=pltpu.VMEM), pl.BlockSpec(memory_space=pltpu.SMEM)
    per = NAO // GROUPS
    return pl.pallas_call(
        place_kernel,
        out_shape=(
            jax.ShapeDtypeStruct((8, NAO * NB * SB), jnp.bfloat16),
            jax.ShapeDtypeStruct((8, OCC), jnp.float32),
        ),
        in_specs=[smem, vmem, vmem],
        out_specs=(vmem, vmem),
        scratch_shapes=[pltpu.VMEM(((per + 2) * NB // 2, 8, LANES), jnp.float32)] * GROUPS,
        compiler_params=pltpu.CompilerParams(vmem_limit_bytes=40 << 20),
        cost_estimate=pl.CostEstimate(flops=1_000_000, bytes_accessed=1_500_000, transcendentals=0),
        name="place",
    )(cols, got, pair_got)


def per_device(tiles, slot_row_block, tile_col, coeff):
    all_cols = lax.all_gather(tile_col, "ao", axis=1, tiled=True)
    got, pair_got = exchange(slot_row_block, tile_col, jnp.transpose(tiles, (1, 0, 2)), coeff.T)
    return place(all_cols, got, pair_got)


def solution(mesh):
    in_specs = (P("aux", "ao", None), P("aux", "ao"), P("aux", "ao"), P("ao", None))
    out_specs = (P(("aux", "ao"), None), P(("aux", "ao"), None))
    return jax.shard_map(per_device, mesh=mesh, in_specs=in_specs, out_specs=out_specs, check_vma=False)
```

```python
import jax
import jax.numpy as jnp
from jax import lax
from jax.experimental import pallas as pl
from jax.experimental.pallas import tpu as pltpu
from jax.sharding import PartitionSpec as P

SB = 64
OCC = 64
NB = 10
NT = 12
QD = 8
SIDE = 8
NAO = SIDE * SIDE
LANES = 128
GROUPS = SIDE
MESH = pl.DeviceIdType.MESH


def lower_half(shape):
    return lax.broadcasted_iota(jnp.int32, shape, len(shape) - 1) < SB


def swap_halves(x):
    return pltpu.roll(x, SB, axis=x.ndim - 1)


def doubled_blocks(coeff_ref, out_ref, first):
    for pair in range(NB // 2):
        x = coeff_ref[:, pair * LANES : (pair + 1) * LANES].astype(jnp.float32)
        y = swap_halves(x)
        low = lower_half(x.shape)
        out_ref[first + 2 * pair] = jnp.where(low, x, y).astype(jnp.bfloat16)
        out_ref[first + 2 * pair + 1] = jnp.where(low, y, x).astype(jnp.bfloat16)


def exchange_kernel(
    rows_hbm, cols_hbm, tiles, coeff_hbm, got, pair_got,
    rows, cols, coeff, raw, turned, send, halves, blocks, near, part, part_got, mid,
    ready, small_sems, load_sems, near_send, near_recv, main_send, main_recv, col_send, col_recv, row_send, row_recv, own_sems,
):
    aux, me = lax.axis_index("aux"), lax.axis_index("ao")
    y, z = me // SIDE, me % SIDE

    barrier = pltpu.get_barrier_semaphore()

    smalls = [
        pltpu.make_async_copy(a, b, small_sems.at[i])
        for i, (a, b) in enumerate(((coeff_hbm, coeff), (rows_hbm, rows), (cols_hbm, cols)))
    ]
    for small in smalls:
        small.start()
    loads = [pltpu.make_async_copy(tiles.at[pl.ds(4 * g, 4)], raw.at[pl.ds(4 * g, 4)], load_sems.at[g]) for g in range(3)]
    for load in loads:
        load.start()

    @pl.loop(1, SIDE)
    def _(k):
        pl.semaphore_signal(barrier, inc=1, device_id=(aux, y * SIDE + (z + k) % SIDE), device_id_type=MESH)
        pl.semaphore_signal(barrier, inc=1, device_id=(aux, (y + k) % SIDE * SIDE + z), device_id_type=MESH)

    for shift in (1, NAO - 1):
        pl.semaphore_signal(barrier, inc=1, device_id=(aux, (me + shift) % NAO), device_id_type=MESH)

    near_copies = [
        pltpu.make_async_remote_copy(
            coeff, near.at[way], near_send.at[way], near_recv.at[way],
            device_id=(aux, (me + shift) % NAO), device_id_type=MESH,
        )
        for way, shift in ((0, 1), (1, NAO - 1))
    ]

    for small in smalls:
        small.wait()
    doubled_blocks(coeff, blocks, NB)

    for g in range(3):
        loads[g].wait()
        for sub in range(2):
            first = 4 * g + 2 * sub
            for side in range(2):
                for k in range(SB // 2):
                    v = raw[first + side, :, k * LANES : (k + 1) * LANES].astype(jnp.float32)
                    w = swap_halves(v)
                    turned[side, pl.ds(16 * k, 8), :] = v if side == 0 else w
                    turned[side, pl.ds(16 * k + 8, 8), :] = w if side == 0 else v
            left = []
            for side in range(2):
                t = first + side
                c = blocks[NB + rows[0, t]]
                left.append(jnp.where(cols[0, t] >= 0, c, jnp.zeros_like(c)))
            left = jnp.where(lower_half(left[0].shape), left[0], left[1])
            low = lower_half((SB, LANES))
            right = []
            for q in range(QD):
                a = turned[0, pl.ds(q, SB, stride=QD), :]
                b = turned[1, pl.ds(q, SB, stride=QD), :]
                right.append(jnp.concatenate([jnp.where(low, a, 0.0), jnp.where(low, 0.0, b)], axis=0).astype(jnp.bfloat16))
            half = jnp.dot(left, jnp.concatenate(right, axis=1), preferred_element_type=jnp.float32).astype(jnp.bfloat16)
            for q in range(QD):
                hq = half[:, q * LANES : (q + 1) * LANES]
                halves[2 * g + sub, pl.ds(q * OCC, OCC), :] = hq
                send[pl.ds(QD * q, QD), g, pl.ds(8 * sub, 8), :] = hq.reshape(SIDE, 8, LANES)
        if g == 0:
            pl.semaphore_wait(barrier, 2 * SIDE)
            for copy in near_copies:
                copy.start()

            @pl.loop(1, SIDE)
            def _(k):
                pl.semaphore_signal(
                    ready.at[SIDE - k], inc=1, device_id=(aux, y * SIDE + (z + k) % SIDE), device_id_type=MESH
                )

    own = pltpu.make_async_copy(send.at[me], got.at[me], own_sems.at[0])
    own.start()

    def ship(dy, dz):
        to = (y + dy) % SIDE * SIDE + (z + dz) % SIDE
        pltpu.make_async_remote_copy(
            send.at[to], got.at[me], main_send, main_recv, device_id=(aux, to), device_id_type=MESH
        ).start()

    @pl.loop(1, SIDE)
    def _(k):
        ship(k, 0)
        ship(0, k)

    for copy in near_copies:
        copy.wait()
    doubled_blocks(near.at[0], blocks, 0)
    doubled_blocks(near.at[1], blocks, 2 * NB)
    total = jnp.zeros((QD * OCC, LANES), jnp.float32)
    for s in range(NT // 2):
        w0 = blocks[jnp.maximum(cols[0, 2 * s], 0)]
        w1 = blocks[jnp.maximum(cols[0, 2 * s + 1], 0)]
        w = jnp.where(lower_half(w0.shape), w0, w1)
        total += lax.dot_general(
            halves[s], jnp.concatenate([w, w], axis=0), (((1,), (1,)), ((), ())), preferred_element_type=jnp.float32
        )
    high = total.astype(jnp.bfloat16)
    rest = (total - high.astype(jnp.float32)).astype(jnp.bfloat16)
    part[:, pl.ds(0, OCC), :] = jnp.where(lower_half(high.shape), high, rest).reshape(QD, OCC, LANES)
    lane = lax.broadcasted_iota(jnp.int32, (16, LANES), 1)
    columns = jnp.zeros((16, LANES), jnp.float32)
    for t in range(NT):
        columns = jnp.where(lane == 16 * z + t, jnp.maximum(cols[0, t], 0).astype(jnp.float32), columns)
    for q in range(QD):
        part[q, pl.ds(OCC, 16), :] = columns.astype(jnp.bfloat16)

    own_part = pltpu.make_async_copy(part.at[y], part_got.at[y], own_sems.at[1])
    own_part.start()

    @pl.loop(1, SIDE)
    def _(k):
        to = (y + k) % SIDE
        pltpu.make_async_remote_copy(
            part.at[to], part_got.at[y], col_send, col_recv, device_id=(aux, to * SIDE + z), device_id_type=MESH
        ).start()

    @pl.loop(1, SIDE)
    def _(k):
        pl.semaphore_wait(ready.at[k], 1)

        @pl.loop(1, SIDE)
        def _(j):
            ship(j, k)

    seven = pl.ds(0, SIDE - 1)
    own_part.wait()
    pltpu.make_async_copy(part_got.at[seven], part_got.at[seven], col_recv).wait()
    arrived = part_got[0].astype(jnp.float32)
    summed, columns = arrived[:OCC], arrived[OCC : OCC + 8]
    row = lax.broadcasted_iota(jnp.int32, columns.shape, 0)
    for k in range(1, SIDE):
        arrived = part_got[k].astype(jnp.float32)
        summed += arrived[:OCC]
        columns = jnp.where(row == k, arrived[OCC : OCC + 8], columns)
    summed += swap_halves(summed)
    mid[:, pl.ds(0, 8), :] = summed.reshape(SIDE, 8, LANES)
    for k in range(SIDE):
        mid[k, pl.ds(8, 8), :] = columns
    own_mid = pltpu.make_async_copy(mid.at[z], pair_got.at[z], own_sems.at[2])
    own_mid.start()

    @pl.loop(1, SIDE)
    def _(k):
        to = (z + k) % SIDE
        pltpu.make_async_remote_copy(
            mid.at[to], pair_got.at[z], row_send, row_recv, device_id=(aux, y * SIDE + to), device_id_type=MESH
        ).start()

    own.wait()
    own_mid.wait()
    most = pl.ds(0, NAO - 1)
    pltpu.make_async_copy(part.at[seven], part.at[seven], col_send).wait()
    pltpu.make_async_copy(mid.at[seven], mid.at[seven], row_send).wait()
    pltpu.make_async_copy(send.at[most], send.at[most], main_send).wait()
    pltpu.make_async_copy(pair_got.at[seven], pair_got.at[seven], row_recv).wait()
    pltpu.make_async_copy(got.at[most], got.at[most], main_recv).wait()


def exchange(rows, cols, tiles, coeff):
    vmem, hbm = pl.BlockSpec(memory_space=pltpu.VMEM), pl.BlockSpec(memory_space=pltpu.HBM)
    dma = pltpu.SemaphoreType.DMA
    bf16, f32 = jnp.bfloat16, jnp.float32
    return pl.pallas_call(
        exchange_kernel,
        out_shape=(
            jax.ShapeDtypeStruct((NAO, 3, 16, LANES), bf16),
            jax.ShapeDtypeStruct((SIDE, 16, LANES), f32),
        ),
        in_specs=[hbm, hbm, hbm, hbm],
        out_specs=(vmem, vmem),
        scratch_shapes=[
            pltpu.SMEM((1, NT), jnp.int32),
            pltpu.SMEM((1, NT), jnp.int32),
            pltpu.VMEM((OCC, NB * SB), bf16),
            pltpu.VMEM((NT, QD, SB * SB), bf16),
            pltpu.VMEM((2, SB * QD, LANES), f32),
            pltpu.VMEM((NAO, 3, 16, LANES), bf16),
            pltpu.VMEM((NT // 2, QD * OCC, LANES), bf16),
            pltpu.VMEM((3 * NB, OCC, LANES), bf16),
            pltpu.VMEM((2, OCC, NB * SB), bf16),
            pltpu.VMEM((QD, OCC + 16, LANES), bf16),
            pltpu.VMEM((SIDE, OCC + 16, LANES), bf16),
            pltpu.VMEM((SIDE, 16, LANES), f32),
            pltpu.SemaphoreType.REGULAR((SIDE,)), dma((3,)), dma((3,)), dma((2,)), dma((2,)), dma, dma, dma, dma, dma, dma, dma((3,)),
        ],
        compiler_params=pltpu.CompilerParams(collective_id=0, has_side_effects=True, vmem_limit_bytes=40 << 20),
        cost_estimate=pl.CostEstimate(flops=200_000_000, bytes_accessed=3_000_000, transcendentals=0),
        name="half_transform_exchange",
    )(rows, cols, tiles, coeff)


def place_kernel(got, pair_got, relaid, pair_ints, cols_vmem, cols, cols_sem, *sums):
    per = NAO // GROUPS
    tiles_per = NB // 2
    zero = jnp.zeros((8, LANES), jnp.float32)
    columns = pair_got[0, pl.ds(8, 8), :]
    for k in range(1, SIDE):
        columns += pair_got[k, pl.ds(8, 8), :]
    cols_vmem[...] = columns.astype(jnp.int32)
    fetch = pltpu.make_async_copy(cols_vmem, cols, cols_sem)
    fetch.start()
    for total in sums:
        total[...] = jnp.zeros(total.shape, jnp.float32)
    half_of = lax.broadcasted_iota(jnp.int32, (8, LANES), 1) // SB
    low = half_of == 0
    fetch.wait()

    @pl.loop(0, per)
    def _(k):
        for s in range(NT // 2):
            for g in range(GROUPS):
                p = g * per + k
                v = got[p, s // 2, pl.ds(8 * (s % 2), 8), :].astype(jnp.float32)
                w = swap_halves(v)
                for side in range(2):
                    both = jnp.where(low, v, w) if side == 0 else jnp.where(low, w, v)
                    c = cols[g, 16 * k + 2 * s + side]
                    at = tiles_per * k + lax.shift_right_logical(c, 1)
                    sums[g][at] += jnp.where(half_of == jnp.bitwise_and(c, 1), both, zero)

    for tile in range(NAO * tiles_per):
        g, local = divmod(tile, per * tiles_per)
        value = sums[g][local + tiles_per]
        if local < tiles_per and g > 0:
            value += sums[g - 1][local + (per + 1) * tiles_per]
        if local >= (per - 1) * tiles_per and g < GROUPS - 1:
            value += sums[g + 1][local - (per - 1) * tiles_per]
        relaid[:, tile * LANES : (tile + 1) * LANES] = value.astype(jnp.bfloat16)

    total = pair_got[0, pl.ds(0, 8), :]
    for k in range(1, SIDE):
        total += pair_got[k, pl.ds(0, 8), :]
    pair_ints[...] = total[:, :OCC]


def place(got, pair_got):
    vmem = pl.BlockSpec(memory_space=pltpu.VMEM)
    per = NAO // GROUPS
    return pl.pallas_call(
        place_kernel,
        out_shape=(
            jax.ShapeDtypeStruct((8, NAO * NB * SB), jnp.bfloat16),
            jax.ShapeDtypeStruct((8, OCC), jnp.float32),
        ),
        in_specs=[vmem, vmem],
        out_specs=(vmem, vmem),
        scratch_shapes=[
            pltpu.VMEM((SIDE, LANES), jnp.int32),
            pltpu.SMEM((SIDE, LANES), jnp.int32),
            pltpu.SemaphoreType.DMA,
            *[pltpu.VMEM(((per + 2) * NB // 2, 8, LANES), jnp.float32)] * GROUPS,
        ],
        compiler_params=pltpu.CompilerParams(vmem_limit_bytes=40 << 20),
        cost_estimate=pl.CostEstimate(flops=1_000_000, bytes_accessed=1_500_000, transcendentals=0),
        name="place",
    )(got, pair_got)


def per_device(tiles, slot_row_block, tile_col, coeff):
    operands = slot_row_block, tile_col, jnp.transpose(tiles, (1, 0, 2)), coeff.T
    got, pair_got = exchange(*(pltpu.with_memory_space_constraint(x, pltpu.HBM) for x in operands))
    return place(got, pair_got)


def solution(mesh):
    in_specs = (P("aux", "ao", None), P("aux", "ao"), P("aux", "ao"), P("ao", None))
    out_specs = (P(("aux", "ao"), None), P(("aux", "ao"), None))
    return jax.shard_map(per_device, mesh=mesh, in_specs=in_specs, out_specs=out_specs, check_vma=False)
```

```python
import jax
import jax.numpy as jnp
from jax import lax
from jax.experimental import pallas as pl
from jax.experimental.pallas import tpu as pltpu
from jax.sharding import PartitionSpec as P

SB = 64
OCC = 64
NB = 10
NT = 12
QD = 8
SIDE = 8
NAO = SIDE * SIDE
LANES = 128
GROUPS = SIDE
MESH = pl.DeviceIdType.MESH
FAR_FIRST = (4, 3, -3, 2, -2, 1, -1)


def lower_half(shape):
    return lax.broadcasted_iota(jnp.int32, shape, len(shape) - 1) < SB


def swap_halves(x):
    return pltpu.roll(x, SB, axis=x.ndim - 1)


def doubled_blocks(coeff_ref, out_ref, first):
    for pair in range(NB // 2):
        x = coeff_ref[:, pair * LANES : (pair + 1) * LANES].astype(jnp.float32)
        y = swap_halves(x)
        low = lower_half(x.shape)
        out_ref[first + 2 * pair] = jnp.where(low, x, y).astype(jnp.bfloat16)
        out_ref[first + 2 * pair + 1] = jnp.where(low, y, x).astype(jnp.bfloat16)


def exchange_kernel(
    rows_hbm, cols_hbm, tiles, coeff_hbm, got, pair_got,
    rows, cols, coeff, raw, turned, send, halves, blocks, near, part, part_got, mid,
    ready, small_sems, load_sems, near_send, near_recv, main_send, main_recv, col_send, col_recv, row_send, row_recv, own_sems,
):
    aux, me = lax.axis_index("aux"), lax.axis_index("ao")
    y, z = me // SIDE, me % SIDE

    barrier = pltpu.get_barrier_semaphore()

    smalls = [
        pltpu.make_async_copy(a, b, small_sems.at[i])
        for i, (a, b) in enumerate(((coeff_hbm, coeff), (rows_hbm, rows), (cols_hbm, cols)))
    ]
    for small in smalls:
        small.start()
    loads = [pltpu.make_async_copy(tiles.at[pl.ds(4 * g, 4)], raw.at[pl.ds(4 * g, 4)], load_sems.at[g]) for g in range(3)]
    for load in loads:
        load.start()

    @pl.loop(1, SIDE)
    def _(k):
        pl.semaphore_signal(barrier, inc=1, device_id=(aux, y * SIDE + (z + k) % SIDE), device_id_type=MESH)
        pl.semaphore_signal(barrier, inc=1, device_id=(aux, (y + k) % SIDE * SIDE + z), device_id_type=MESH)

    for shift in (1, NAO - 1):
        pl.semaphore_signal(barrier, inc=1, device_id=(aux, (me + shift) % NAO), device_id_type=MESH)

    near_copies = [
        pltpu.make_async_remote_copy(
            coeff, near.at[way], near_send.at[way], near_recv.at[way],
            device_id=(aux, (me + shift) % NAO), device_id_type=MESH,
        )
        for way, shift in ((0, 1), (1, NAO - 1))
    ]

    for small in smalls:
        small.wait()
    doubled_blocks(coeff, blocks, NB)

    for g in range(3):
        loads[g].wait()
        for sub in range(2):
            first = 4 * g + 2 * sub
            for side in range(2):
                for k in range(SB // 2):
                    v = raw[first + side, :, k * LANES : (k + 1) * LANES].astype(jnp.float32)
                    w = swap_halves(v)
                    turned[side, pl.ds(16 * k, 8), :] = v if side == 0 else w
                    turned[side, pl.ds(16 * k + 8, 8), :] = w if side == 0 else v
            left = []
            for side in range(2):
                t = first + side
                c = blocks[NB + rows[0, t]]
                left.append(jnp.where(cols[0, t] >= 0, c, jnp.zeros_like(c)))
            left = jnp.where(lower_half(left[0].shape), left[0], left[1])
            low = lower_half((SB, LANES))
            right = []
            for q in range(QD):
                a = turned[0, pl.ds(q, SB, stride=QD), :]
                b = turned[1, pl.ds(q, SB, stride=QD), :]
                right.append(jnp.concatenate([jnp.where(low, a, 0.0), jnp.where(low, 0.0, b)], axis=0).astype(jnp.bfloat16))
            half = jnp.dot(left, jnp.concatenate(right, axis=1), preferred_element_type=jnp.float32).astype(jnp.bfloat16)
            for q in range(QD):
                hq = half[:, q * LANES : (q + 1) * LANES]
                halves[2 * g + sub, pl.ds(q * OCC, OCC), :] = hq
                send[pl.ds(QD * q, QD), g, pl.ds(8 * sub, 8), :] = hq.reshape(SIDE, 8, LANES)
        if g == 0:
            pl.semaphore_wait(barrier, 2 * SIDE)
            for copy in near_copies:
                copy.start()

            @pl.loop(1, SIDE)
            def _(k):
                pl.semaphore_signal(
                    ready.at[SIDE - k], inc=1, device_id=(aux, y * SIDE + (z + k) % SIDE), device_id_type=MESH
                )

    own = pltpu.make_async_copy(send.at[me], got.at[me], own_sems.at[0])
    own.start()

    def ship(dy, dz):
        to = (y + dy + SIDE) % SIDE * SIDE + (z + dz + SIDE) % SIDE
        pltpu.make_async_remote_copy(
            send.at[to], got.at[me], main_send, main_recv, device_id=(aux, to), device_id_type=MESH
        ).start()

    for far in FAR_FIRST:
        ship(far, 0)
        ship(0, far)

    def ship_column(k):
        pl.semaphore_wait(ready.at[k % SIDE], 1)
        for j in FAR_FIRST:
            ship(j, k)

    ship_column(FAR_FIRST[0])

    for copy in near_copies:
        copy.wait()
    doubled_blocks(near.at[0], blocks, 0)
    doubled_blocks(near.at[1], blocks, 2 * NB)
    total = jnp.zeros((QD * OCC, LANES), jnp.float32)
    for s in range(NT // 2):
        w0 = blocks[jnp.maximum(cols[0, 2 * s], 0)]
        w1 = blocks[jnp.maximum(cols[0, 2 * s + 1], 0)]
        w = jnp.where(lower_half(w0.shape), w0, w1)
        total += lax.dot_general(
            halves[s], jnp.concatenate([w, w], axis=0), (((1,), (1,)), ((), ())), preferred_element_type=jnp.float32
        )
    high = total.astype(jnp.bfloat16)
    rest = (total - high.astype(jnp.float32)).astype(jnp.bfloat16)
    part[:, pl.ds(0, OCC), :] = jnp.where(lower_half(high.shape), high, rest).reshape(QD, OCC, LANES)
    lane = lax.broadcasted_iota(jnp.int32, (16, LANES), 1)
    columns = jnp.zeros((16, LANES), jnp.float32)
    for t in range(NT):
        columns = jnp.where(lane == 16 * z + t, jnp.maximum(cols[0, t], 0).astype(jnp.float32), columns)
    for q in range(QD):
        part[q, pl.ds(OCC, 16), :] = columns.astype(jnp.bfloat16)

    own_part = pltpu.make_async_copy(part.at[y], part_got.at[y], own_sems.at[1])
    own_part.start()

    @pl.loop(1, SIDE)
    def _(k):
        to = (y + k) % SIDE
        pltpu.make_async_remote_copy(
            part.at[to], part_got.at[y], col_send, col_recv, device_id=(aux, to * SIDE + z), device_id_type=MESH
        ).start()

    for k in FAR_FIRST[1:]:
        ship_column(k)

    seven = pl.ds(0, SIDE - 1)
    own_part.wait()
    pltpu.make_async_copy(part_got.at[seven], part_got.at[seven], col_recv).wait()
    arrived = part_got[0].astype(jnp.float32)
    summed, columns = arrived[:OCC], arrived[OCC : OCC + 8]
    row = lax.broadcasted_iota(jnp.int32, columns.shape, 0)
    for k in range(1, SIDE):
        arrived = part_got[k].astype(jnp.float32)
        summed += arrived[:OCC]
        columns = jnp.where(row == k, arrived[OCC : OCC + 8], columns)
    summed += swap_halves(summed)
    mid[:, pl.ds(0, 8), :] = summed.reshape(SIDE, 8, LANES)
    for k in range(SIDE):
        mid[k, pl.ds(8, 8), :] = columns
    own_mid = pltpu.make_async_copy(mid.at[z], pair_got.at[z], own_sems.at[2])
    own_mid.start()

    @pl.loop(1, SIDE)
    def _(k):
        to = (z + k) % SIDE
        pltpu.make_async_remote_copy(
            mid.at[to], pair_got.at[z], row_send, row_recv, device_id=(aux, y * SIDE + to), device_id_type=MESH
        ).start()

    own.wait()
    own_mid.wait()
    most = pl.ds(0, NAO - 1)
    pltpu.make_async_copy(part.at[seven], part.at[seven], col_send).wait()
    pltpu.make_async_copy(mid.at[seven], mid.at[seven], row_send).wait()
    pltpu.make_async_copy(send.at[most], send.at[most], main_send).wait()
    pltpu.make_async_copy(pair_got.at[seven], pair_got.at[seven], row_recv).wait()
    pltpu.make_async_copy(got.at[most], got.at[most], main_recv).wait()


def exchange(rows, cols, tiles, coeff):
    vmem, hbm = pl.BlockSpec(memory_space=pltpu.VMEM), pl.BlockSpec(memory_space=pltpu.HBM)
    dma = pltpu.SemaphoreType.DMA
    bf16, f32 = jnp.bfloat16, jnp.float32
    return pl.pallas_call(
        exchange_kernel,
        out_shape=(
            jax.ShapeDtypeStruct((NAO, 3, 16, LANES), bf16),
            jax.ShapeDtypeStruct((SIDE, 16, LANES), f32),
        ),
        in_specs=[hbm, hbm, hbm, hbm],
        out_specs=(vmem, vmem),
        scratch_shapes=[
            pltpu.SMEM((1, NT), jnp.int32),
            pltpu.SMEM((1, NT), jnp.int32),
            pltpu.VMEM((OCC, NB * SB), bf16),
            pltpu.VMEM((NT, QD, SB * SB), bf16),
            pltpu.VMEM((2, SB * QD, LANES), f32),
            pltpu.VMEM((NAO, 3, 16, LANES), bf16),
            pltpu.VMEM((NT // 2, QD * OCC, LANES), bf16),
            pltpu.VMEM((3 * NB, OCC, LANES), bf16),
            pltpu.VMEM((2, OCC, NB * SB), bf16),
            pltpu.VMEM((QD, OCC + 16, LANES), bf16),
            pltpu.VMEM((SIDE, OCC + 16, LANES), bf16),
            pltpu.VMEM((SIDE, 16, LANES), f32),
            pltpu.SemaphoreType.REGULAR((SIDE,)), dma((3,)), dma((3,)), dma((2,)), dma((2,)), dma, dma, dma, dma, dma, dma, dma((3,)),
        ],
        compiler_params=pltpu.CompilerParams(collective_id=0, has_side_effects=True, vmem_limit_bytes=40 << 20),
        cost_estimate=pl.CostEstimate(flops=200_000_000, bytes_accessed=3_000_000, transcendentals=0),
        name="half_transform_exchange",
    )(rows, cols, tiles, coeff)


def place_kernel(got, pair_got, relaid, pair_ints, cols_vmem, cols, cols_sem, *sums):
    per = NAO // GROUPS
    tiles_per = NB // 2
    zero = jnp.zeros((8, LANES), jnp.float32)
    columns = pair_got[0, pl.ds(8, 8), :]
    for k in range(1, SIDE):
        columns += pair_got[k, pl.ds(8, 8), :]
    cols_vmem[...] = columns.astype(jnp.int32)
    fetch = pltpu.make_async_copy(cols_vmem, cols, cols_sem)
    fetch.start()
    for total in sums:
        total[...] = jnp.zeros(total.shape, jnp.float32)
    half_of = lax.broadcasted_iota(jnp.int32, (8, LANES), 1) // SB
    low = half_of == 0
    fetch.wait()

    @pl.loop(0, per)
    def _(k):
        for s in range(NT // 2):
            for g in range(GROUPS):
                p = g * per + k
                v = got[p, s // 2, pl.ds(8 * (s % 2), 8), :].astype(jnp.float32)
                w = swap_halves(v)
                for side in range(2):
                    both = jnp.where(low, v, w) if side == 0 else jnp.where(low, w, v)
                    c = cols[g, 16 * k + 2 * s + side]
                    at = tiles_per * k + lax.shift_right_logical(c, 1)
                    sums[g][at] += jnp.where(half_of == jnp.bitwise_and(c, 1), both, zero)

    for tile in range(NAO * tiles_per):
        g, local = divmod(tile, per * tiles_per)
        value = sums[g][local + tiles_per]
        if local < tiles_per and g > 0:
            value += sums[g - 1][local + (per + 1) * tiles_per]
        if local >= (per - 1) * tiles_per and g < GROUPS - 1:
            value += sums[g + 1][local - (per - 1) * tiles_per]
        relaid[:, tile * LANES : (tile + 1) * LANES] = value.astype(jnp.bfloat16)

    total = pair_got[0, pl.ds(0, 8), :]
    for k in range(1, SIDE):
        total += pair_got[k, pl.ds(0, 8), :]
    pair_ints[...] = total[:, :OCC]


def place(got, pair_got):
    vmem = pl.BlockSpec(memory_space=pltpu.VMEM)
    per = NAO // GROUPS
    return pl.pallas_call(
        place_kernel,
        out_shape=(
            jax.ShapeDtypeStruct((8, NAO * NB * SB), jnp.bfloat16),
            jax.ShapeDtypeStruct((8, OCC), jnp.float32),
        ),
        in_specs=[vmem, vmem],
        out_specs=(vmem, vmem),
        scratch_shapes=[
            pltpu.VMEM((SIDE, LANES), jnp.int32),
            pltpu.SMEM((SIDE, LANES), jnp.int32),
            pltpu.SemaphoreType.DMA,
            *[pltpu.VMEM(((per + 2) * NB // 2, 8, LANES), jnp.float32)] * GROUPS,
        ],
        compiler_params=pltpu.CompilerParams(vmem_limit_bytes=40 << 20),
        cost_estimate=pl.CostEstimate(flops=1_000_000, bytes_accessed=1_500_000, transcendentals=0),
        name="place",
    )(got, pair_got)


def per_device(tiles, slot_row_block, tile_col, coeff):
    operands = slot_row_block, tile_col, jnp.transpose(tiles, (1, 0, 2)), coeff.T
    got, pair_got = exchange(*(pltpu.with_memory_space_constraint(x, pltpu.HBM) for x in operands))
    return place(got, pair_got)


def solution(mesh):
    in_specs = (P("aux", "ao", None), P("aux", "ao"), P("aux", "ao"), P("ao", None))
    out_specs = (P(("aux", "ao"), None), P(("aux", "ao"), None))
    return jax.shard_map(per_device, mesh=mesh, in_specs=in_specs, out_specs=out_specs, check_vma=False)
```

```python
import jax
import jax.numpy as jnp
from jax import lax
from jax.experimental import pallas as pl
from jax.experimental.pallas import tpu as pltpu
from jax.sharding import PartitionSpec as P

SB = 64
OCC = 64
NB = 10
NT = 12
QD = 8
SIDE = 8
NAO = SIDE * SIDE
LANES = 128
GROUPS = SIDE
MESH = pl.DeviceIdType.MESH
REACH = SIDE


def offsets_at(hops):
    near = range(1 - SIDE // 2, SIDE // 2 + 1)
    found = []
    for start in ((a, b) for a in near for b in near):
        a, b = start
        for _ in range(4):
            if abs(a) + abs(b) == hops and (a, b) not in found:
                found.append((a, b))
            a, b = (-b if b != SIDE // 2 else b), a
    return found


def lower_half(shape):
    return lax.broadcasted_iota(jnp.int32, shape, len(shape) - 1) < SB


def swap_halves(x):
    return pltpu.roll(x, SB, axis=x.ndim - 1)


def doubled_blocks(coeff_ref, out_ref, first):
    for pair in range(NB // 2):
        x = coeff_ref[:, pair * LANES : (pair + 1) * LANES].astype(jnp.float32)
        y = swap_halves(x)
        low = lower_half(x.shape)
        out_ref[first + 2 * pair] = jnp.where(low, x, y).astype(jnp.bfloat16)
        out_ref[first + 2 * pair + 1] = jnp.where(low, y, x).astype(jnp.bfloat16)


def exchange_kernel(
    rows_hbm, cols_hbm, tiles, coeff_hbm, got, pair_got,
    rows, cols, coeff, raw, turned, send, halves, blocks, near, part, part_got, mid, col_row, col_rows,
    circles, small_sems, load_sems, near_send, near_recv, main_send, main_recv, col_send, col_recv, row_send, row_recv, list_send, list_recv, own_sems,
):
    aux, me = lax.axis_index("aux"), lax.axis_index("ao")
    y, z = me // SIDE, me % SIDE

    barrier = pltpu.get_barrier_semaphore()

    smalls = [
        pltpu.make_async_copy(a, b, small_sems.at[i])
        for i, (a, b) in enumerate(((coeff_hbm, coeff), (rows_hbm, rows), (cols_hbm, cols)))
    ]
    for small in smalls:
        small.start()
    loads = [pltpu.make_async_copy(tiles.at[pl.ds(4 * g, 4)], raw.at[pl.ds(4 * g, 4)], load_sems.at[g]) for g in range(3)]
    for load in loads:
        load.start()

    def beside(dy, dz):
        return (y + dy + SIDE) % SIDE * SIDE + (z + dz + SIDE) % SIDE

    def tell(semaphore):
        for offset in offsets_at(1):
            pl.semaphore_signal(semaphore, inc=1, device_id=(aux, beside(*offset)), device_id_type=MESH)

    def widen(circle):
        if circle > 1:
            pl.semaphore_wait(circles.at[circle - 1], 4)
        if circle < REACH:
            tell(circles.at[circle])

    tell(barrier)
    for shift in (1, NAO - 1):
        pl.semaphore_signal(barrier, inc=1, device_id=(aux, (me + shift) % NAO), device_id_type=MESH)

    near_copies = [
        pltpu.make_async_remote_copy(
            coeff, near.at[way], near_send.at[way], near_recv.at[way],
            device_id=(aux, (me + shift) % NAO), device_id_type=MESH,
        )
        for way, shift in ((0, 1), (1, NAO - 1))
    ]

    for small in smalls:
        small.wait()
    doubled_blocks(coeff, blocks, NB)

    for g in range(3):
        loads[g].wait()
        for sub in range(2):
            first = 4 * g + 2 * sub
            for side in range(2):
                for k in range(SB // 2):
                    v = raw[first + side, :, k * LANES : (k + 1) * LANES].astype(jnp.float32)
                    w = swap_halves(v)
                    turned[side, pl.ds(16 * k, 8), :] = v if side == 0 else w
                    turned[side, pl.ds(16 * k + 8, 8), :] = w if side == 0 else v
            left = []
            for side in range(2):
                t = first + side
                c = blocks[NB + rows[0, t]]
                left.append(jnp.where(cols[0, t] >= 0, c, jnp.zeros_like(c)))
            left = jnp.where(lower_half(left[0].shape), left[0], left[1])
            low = lower_half((SB, LANES))
            right = []
            for q in range(QD):
                a = turned[0, pl.ds(q, SB, stride=QD), :]
                b = turned[1, pl.ds(q, SB, stride=QD), :]
                right.append(jnp.concatenate([jnp.where(low, a, 0.0), jnp.where(low, 0.0, b)], axis=0).astype(jnp.bfloat16))
            half = jnp.dot(left, jnp.concatenate(right, axis=1), preferred_element_type=jnp.float32).astype(jnp.bfloat16)
            for q in range(QD):
                hq = half[:, q * LANES : (q + 1) * LANES]
                halves[2 * g + sub, pl.ds(q * OCC, OCC), :] = hq
                send[pl.ds(QD * q, QD), g, pl.ds(8 * sub, 8), :] = hq.reshape(SIDE, 8, LANES)
        if g == 0:
            pl.semaphore_wait(barrier, 6)
            for copy in near_copies:
                copy.start()
        if g < 2:
            widen(g + 1)

    own = pltpu.make_async_copy(send.at[me], got.at[me], own_sems.at[0])
    own.start()

    def ship_circle(hops):
        if hops > 2:
            widen(hops)
        for offset in offsets_at(hops):
            to = beside(*offset)
            pltpu.make_async_remote_copy(
                send.at[to], got.at[me], main_send, main_recv, device_id=(aux, to), device_id_type=MESH
            ).start()

    for hops in range(1, 5):
        ship_circle(hops)

    for copy in near_copies:
        copy.wait()
    doubled_blocks(near.at[0], blocks, 0)
    doubled_blocks(near.at[1], blocks, 2 * NB)
    total = jnp.zeros((QD * OCC, LANES), jnp.float32)
    for s in range(NT // 2):
        w0 = blocks[jnp.maximum(cols[0, 2 * s], 0)]
        w1 = blocks[jnp.maximum(cols[0, 2 * s + 1], 0)]
        w = jnp.where(lower_half(w0.shape), w0, w1)
        total += lax.dot_general(
            halves[s], jnp.concatenate([w, w], axis=0), (((1,), (1,)), ((), ())), preferred_element_type=jnp.float32
        )
    high = total.astype(jnp.bfloat16)
    rest = (total - high.astype(jnp.float32)).astype(jnp.bfloat16)
    part[...] = jnp.where(lower_half(high.shape), high, rest).reshape(QD, OCC, LANES)
    lane = lax.broadcasted_iota(jnp.int32, (1, LANES), 1)
    columns = jnp.zeros((1, LANES), jnp.float32)
    for t in range(NT):
        here = lane == SB + 16 * (z % 4) + t
        columns = jnp.where(here, jnp.maximum(cols[0, t], 0).astype(jnp.float32), columns)
    col_row[...] = columns

    own_part = pltpu.make_async_copy(part.at[y], part_got.at[y], own_sems.at[1])
    own_part.start()
    own_row = pltpu.make_async_copy(col_row, col_rows.at[y], own_sems.at[3])
    own_row.start()

    @pl.loop(1, SIDE)
    def _(k):
        to = (y + k) % SIDE
        pltpu.make_async_remote_copy(
            part.at[to], part_got.at[y], col_send, col_recv, device_id=(aux, to * SIDE + z), device_id_type=MESH
        ).start()
        pltpu.make_async_remote_copy(
            col_row, col_rows.at[y], list_send, list_recv, device_id=(aux, to * SIDE + z), device_id_type=MESH
        ).start()

    for hops in range(5, 7):
        ship_circle(hops)

    seven = pl.ds(0, SIDE - 1)
    own_part.wait()
    pltpu.make_async_copy(part_got.at[seven], part_got.at[seven], col_recv).wait()
    own_row.wait()
    pltpu.make_async_copy(col_rows.at[seven], col_rows.at[seven], list_recv).wait()
    summed = part_got[0].astype(jnp.float32)
    for k in range(1, SIDE):
        summed += part_got[k].astype(jnp.float32)
    summed += swap_halves(summed)
    row = lax.broadcasted_iota(jnp.int32, (8, LANES), 0)
    columns = jnp.zeros((8, LANES), jnp.float32)
    for k in range(SIDE):
        columns = jnp.where(row == k, col_rows[k], columns)
    for k in range(SIDE):
        mid[k] = jnp.where(lower_half((8, LANES)), summed[8 * k : 8 * k + 8], columns)
    own_mid = pltpu.make_async_copy(mid.at[z], pair_got.at[z], own_sems.at[2])
    own_mid.start()

    @pl.loop(1, SIDE)
    def _(k):
        to = (z + k) % SIDE
        pltpu.make_async_remote_copy(
            mid.at[to], pair_got.at[z], row_send, row_recv, device_id=(aux, y * SIDE + to), device_id_type=MESH
        ).start()

    for hops in range(7, REACH + 1):
        ship_circle(hops)

    own.wait()
    own_mid.wait()
    most = pl.ds(0, NAO - 1)
    pltpu.make_async_copy(part.at[seven], part.at[seven], col_send).wait()
    pltpu.make_async_copy(col_rows.at[seven], col_rows.at[seven], list_send).wait()
    pltpu.make_async_copy(mid.at[seven], mid.at[seven], row_send).wait()
    pltpu.make_async_copy(send.at[most], send.at[most], main_send).wait()
    pltpu.make_async_copy(pair_got.at[seven], pair_got.at[seven], row_recv).wait()
    pltpu.make_async_copy(got.at[most], got.at[most], main_recv).wait()


def exchange(rows, cols, tiles, coeff):
    vmem, hbm = pl.BlockSpec(memory_space=pltpu.VMEM), pl.BlockSpec(memory_space=pltpu.HBM)
    dma = pltpu.SemaphoreType.DMA
    bf16, f32 = jnp.bfloat16, jnp.float32
    return pl.pallas_call(
        exchange_kernel,
        out_shape=(
            jax.ShapeDtypeStruct((NAO, 3, 16, LANES), bf16),
            jax.ShapeDtypeStruct((SIDE, 8, LANES), f32),
        ),
        in_specs=[hbm, hbm, hbm, hbm],
        out_specs=(vmem, vmem),
        scratch_shapes=[
            pltpu.SMEM((1, NT), jnp.int32),
            pltpu.SMEM((1, NT), jnp.int32),
            pltpu.VMEM((OCC, NB * SB), bf16),
            pltpu.VMEM((NT, QD, SB * SB), bf16),
            pltpu.VMEM((2, SB * QD, LANES), f32),
            pltpu.VMEM((NAO, 3, 16, LANES), bf16),
            pltpu.VMEM((NT // 2, QD * OCC, LANES), bf16),
            pltpu.VMEM((3 * NB, OCC, LANES), bf16),
            pltpu.VMEM((2, OCC, NB * SB), bf16),
            pltpu.VMEM((QD, OCC, LANES), bf16),
            pltpu.VMEM((SIDE, OCC, LANES), bf16),
            pltpu.VMEM((SIDE, 8, LANES), f32),
            pltpu.VMEM((1, LANES), f32),
            pltpu.VMEM((SIDE, 1, LANES), f32),
            pltpu.SemaphoreType.REGULAR((SIDE,)), dma((3,)), dma((3,)), dma((2,)), dma((2,)), dma, dma, dma, dma, dma, dma, dma, dma, dma((4,)),
        ],
        compiler_params=pltpu.CompilerParams(collective_id=0, has_side_effects=True, vmem_limit_bytes=40 << 20),
        cost_estimate=pl.CostEstimate(flops=200_000_000, bytes_accessed=3_000_000, transcendentals=0),
        name="half_transform_exchange",
    )(rows, cols, tiles, coeff)


def place_kernel(got, pair_got, relaid, pair_ints, rows_vmem, rows, rows_sem, *sums):
    per = NAO // GROUPS
    low = lower_half((8, LANES))
    total, later = pair_got[0], pair_got[SIDE // 2]
    for k in range(1, SIDE // 2):
        total += pair_got[k]
        later += pair_got[SIDE // 2 + k]
    source = lax.broadcasted_iota(jnp.int32, (8, LANES), 1) // 16
    rows_vmem[...] = 8 * (jnp.where(low, swap_halves(total), later).astype(jnp.int32) + NB * source)
    fetch = pltpu.make_async_copy(rows_vmem, rows, rows_sem)
    fetch.start()
    pair_ints[...] = (total + later)[:, :OCC]
    for part in sums:
        part[...] = jnp.zeros(part.shape, jnp.float32)
    fetch.wait()

    @pl.loop(0, per)
    def _(k):
        for s in range(NT // 2):
            for g in range(GROUPS):
                v = got[g * per + k, s // 2, pl.ds(8 * (s % 2), 8), :].astype(jnp.float32)
                for side in range(2):
                    at = pl.ds(pl.multiple_of(rows[g, 16 * k + 2 * s + side], 8), 8)
                    sums[g][at, :] += jnp.where(low, v, 0.0) if side == 0 else jnp.where(low, 0.0, v)

    def block(b):
        g, local = divmod(b, per * NB)

        def at(i):
            return pl.ds(8 * i, 8)

        value = sums[g][at(local + NB), :]
        if local < NB and g > 0:
            value += sums[g - 1][at(local + (per + 1) * NB), :]
        if local >= (per - 1) * NB and g < GROUPS - 1:
            value += sums[g + 1][at(local - (per - 1) * NB), :]
        return value

    for tile in range(NAO * NB // 2):
        a, b = block(2 * tile), block(2 * tile + 1)
        value = jnp.where(low, a, b) + swap_halves(jnp.where(low, b, a))
        relaid[:, tile * LANES : (tile + 1) * LANES] = value.astype(jnp.bfloat16)


def place(got, pair_got):
    vmem = pl.BlockSpec(memory_space=pltpu.VMEM)
    per = NAO // GROUPS
    return pl.pallas_call(
        place_kernel,
        out_shape=(
            jax.ShapeDtypeStruct((8, NAO * NB * SB), jnp.bfloat16),
            jax.ShapeDtypeStruct((8, OCC), jnp.float32),
        ),
        in_specs=[vmem, vmem],
        out_specs=(vmem, vmem),
        scratch_shapes=[
            pltpu.VMEM((SIDE, LANES), jnp.int32),
            pltpu.SMEM((SIDE, LANES), jnp.int32),
            pltpu.SemaphoreType.DMA,
            *[pltpu.VMEM(((per + 2) * NB * 8, LANES), jnp.float32)] * GROUPS,
        ],
        compiler_params=pltpu.CompilerParams(vmem_limit_bytes=40 << 20),
        cost_estimate=pl.CostEstimate(flops=1_000_000, bytes_accessed=1_500_000, transcendentals=0),
        name="place",
    )(got, pair_got)


def per_device(tiles, slot_row_block, tile_col, coeff):
    operands = slot_row_block, tile_col, jnp.transpose(tiles, (1, 0, 2)), coeff.T
    got, pair_got = exchange(*(pltpu.with_memory_space_constraint(x, pltpu.HBM) for x in operands))
    return place(got, pair_got)


def solution(mesh):
    in_specs = (P("aux", "ao", None), P("aux", "ao"), P("aux", "ao"), P("ao", None))
    out_specs = (P(("aux", "ao"), None), P(("aux", "ao"), None))
    return jax.shard_map(per_device, mesh=mesh, in_specs=in_specs, out_specs=out_specs, check_vma=False)
```

```python
import jax
import jax.numpy as jnp
from jax import lax
from jax.experimental import pallas as pl
from jax.experimental.pallas import tpu as pltpu
from jax.sharding import PartitionSpec as P

SB = 64
OCC = 64
NB = 10
NT = 12
QD = 8
SIDE = 8
NAO = SIDE * SIDE
LANES = 128
GROUPS = SIDE
MESH = pl.DeviceIdType.MESH
FAR_FIRST = (4, 3, -3, 2, -2, 1, -1)


def lower_half(shape):
    return lax.broadcasted_iota(jnp.int32, shape, len(shape) - 1) < SB


def swap_halves(x):
    return pltpu.roll(x, SB, axis=x.ndim - 1)


def doubled_blocks(coeff_ref, out_ref, first):
    for pair in range(NB // 2):
        x = coeff_ref[:, pair * LANES : (pair + 1) * LANES].astype(jnp.float32)
        y = swap_halves(x)
        low = lower_half(x.shape)
        out_ref[first + 2 * pair] = jnp.where(low, x, y).astype(jnp.bfloat16)
        out_ref[first + 2 * pair + 1] = jnp.where(low, y, x).astype(jnp.bfloat16)


def exchange_kernel(
    rows_hbm, cols_hbm, tiles, coeff_hbm, got, pair_got,
    rows, cols, coeff, raw, turned, send, halves, blocks, near, part, part_got, mid, col_row, col_rows,
    ready, small_sems, load_sems, near_send, near_recv, main_send, main_recv, col_send, col_recv, row_send, row_recv, list_send, list_recv, own_sems,
):
    aux, me = lax.axis_index("aux"), lax.axis_index("ao")
    y, z = me // SIDE, me % SIDE

    barrier = pltpu.get_barrier_semaphore()

    smalls = [
        pltpu.make_async_copy(a, b, small_sems.at[i])
        for i, (a, b) in enumerate(((coeff_hbm, coeff), (rows_hbm, rows), (cols_hbm, cols)))
    ]
    for small in smalls:
        small.start()
    loads = [pltpu.make_async_copy(tiles.at[pl.ds(4 * g, 4)], raw.at[pl.ds(4 * g, 4)], load_sems.at[g]) for g in range(3)]
    for load in loads:
        load.start()

    @pl.loop(1, SIDE)
    def _(k):
        pl.semaphore_signal(barrier, inc=1, device_id=(aux, y * SIDE + (z + k) % SIDE), device_id_type=MESH)
        pl.semaphore_signal(barrier, inc=1, device_id=(aux, (y + k) % SIDE * SIDE + z), device_id_type=MESH)

    for shift in (1, NAO - 1):
        pl.semaphore_signal(barrier, inc=1, device_id=(aux, (me + shift) % NAO), device_id_type=MESH)

    near_copies = [
        pltpu.make_async_remote_copy(
            coeff, near.at[way], near_send.at[way], near_recv.at[way],
            device_id=(aux, (me + shift) % NAO), device_id_type=MESH,
        )
        for way, shift in ((0, 1), (1, NAO - 1))
    ]

    for small in smalls:
        small.wait()
    doubled_blocks(coeff, blocks, NB)

    for g in range(3):
        loads[g].wait()
        for sub in range(2):
            first = 4 * g + 2 * sub
            for side in range(2):
                for k in range(SB // 2):
                    v = raw[first + side, :, k * LANES : (k + 1) * LANES].astype(jnp.float32)
                    w = swap_halves(v)
                    turned[side, pl.ds(16 * k, 8), :] = v if side == 0 else w
                    turned[side, pl.ds(16 * k + 8, 8), :] = w if side == 0 else v
            left = []
            for side in range(2):
                t = first + side
                c = blocks[NB + rows[0, t]]
                left.append(jnp.where(cols[0, t] >= 0, c, jnp.zeros_like(c)))
            left = jnp.where(lower_half(left[0].shape), left[0], left[1])
            low = lower_half((SB, LANES))
            right = []
            for q in range(QD):
                a = turned[0, pl.ds(q, SB, stride=QD), :]
                b = turned[1, pl.ds(q, SB, stride=QD), :]
                right.append(jnp.concatenate([jnp.where(low, a, 0.0), jnp.where(low, 0.0, b)], axis=0).astype(jnp.bfloat16))
            half = jnp.dot(left, jnp.concatenate(right, axis=1), preferred_element_type=jnp.float32).astype(jnp.bfloat16)
            for q in range(QD):
                hq = half[:, q * LANES : (q + 1) * LANES]
                halves[2 * g + sub, pl.ds(q * OCC, OCC), :] = hq
                send[pl.ds(QD * q, QD), g, pl.ds(8 * sub, 8), :] = hq.reshape(SIDE, 8, LANES)
        if g == 0:
            pl.semaphore_wait(barrier, 2 * SIDE)
            for copy in near_copies:
                copy.start()

            @pl.loop(1, SIDE)
            def _(k):
                pl.semaphore_signal(
                    ready.at[SIDE - k], inc=1, device_id=(aux, y * SIDE + (z + k) % SIDE), device_id_type=MESH
                )

    own = pltpu.make_async_copy(send.at[me], got.at[me], own_sems.at[0])
    own.start()

    def ship(dy, dz):
        to = (y + dy + SIDE) % SIDE * SIDE + (z + dz + SIDE) % SIDE
        pltpu.make_async_remote_copy(
            send.at[to], got.at[me], main_send, main_recv, device_id=(aux, to), device_id_type=MESH
        ).start()

    for far in FAR_FIRST:
        ship(far, 0)
        ship(0, far)

    def ship_column(k):
        pl.semaphore_wait(ready.at[k % SIDE], 1)
        for j in FAR_FIRST:
            ship(j, k)

    for k in FAR_FIRST[:1]:
        ship_column(k)

    for copy in near_copies:
        copy.wait()
    doubled_blocks(near.at[0], blocks, 0)
    doubled_blocks(near.at[1], blocks, 2 * NB)
    total = jnp.zeros((QD * OCC, LANES), jnp.float32)
    for s in range(NT // 2):
        w0 = blocks[jnp.maximum(cols[0, 2 * s], 0)]
        w1 = blocks[jnp.maximum(cols[0, 2 * s + 1], 0)]
        w = jnp.where(lower_half(w0.shape), w0, w1)
        total += lax.dot_general(
            halves[s], jnp.concatenate([w, w], axis=0), (((1,), (1,)), ((), ())), preferred_element_type=jnp.float32
        )
    high = total.astype(jnp.bfloat16)
    rest = (total - high.astype(jnp.float32)).astype(jnp.bfloat16)
    part[...] = jnp.where(lower_half(high.shape), high, rest).reshape(QD, OCC, LANES)
    lane = lax.broadcasted_iota(jnp.int32, (1, LANES), 1)
    columns = jnp.zeros((1, LANES), jnp.float32)
    for t in range(NT):
        here = lane == SB + 16 * (z % 4) + t
        columns = jnp.where(here, jnp.maximum(cols[0, t], 0).astype(jnp.float32), columns)
    col_row[...] = columns

    own_part = pltpu.make_async_copy(part.at[y], part_got.at[y], own_sems.at[1])
    own_part.start()
    own_row = pltpu.make_async_copy(col_row, col_rows.at[y], own_sems.at[3])
    own_row.start()

    @pl.loop(1, SIDE)
    def _(k):
        to = (y + k) % SIDE
        pltpu.make_async_remote_copy(
            part.at[to], part_got.at[y], col_send, col_recv, device_id=(aux, to * SIDE + z), device_id_type=MESH
        ).start()
        pltpu.make_async_remote_copy(
            col_row, col_rows.at[y], list_send, list_recv, device_id=(aux, to * SIDE + z), device_id_type=MESH
        ).start()

    for k in FAR_FIRST[1:5]:
        ship_column(k)

    seven = pl.ds(0, SIDE - 1)
    own_part.wait()
    pltpu.make_async_copy(part_got.at[seven], part_got.at[seven], col_recv).wait()
    own_row.wait()
    pltpu.make_async_copy(col_rows.at[seven], col_rows.at[seven], list_recv).wait()
    summed = part_got[0].astype(jnp.float32)
    for k in range(1, SIDE):
        summed += part_got[k].astype(jnp.float32)
    summed += swap_halves(summed)
    row = lax.broadcasted_iota(jnp.int32, (8, LANES), 0)
    columns = jnp.zeros((8, LANES), jnp.float32)
    for k in range(SIDE):
        columns = jnp.where(row == k, col_rows[k], columns)
    for k in range(SIDE):
        mid[k] = jnp.where(lower_half((8, LANES)), summed[8 * k : 8 * k + 8], columns)
    own_mid = pltpu.make_async_copy(mid.at[z], pair_got.at[z], own_sems.at[2])
    own_mid.start()

    @pl.loop(1, SIDE)
    def _(k):
        to = (z + k) % SIDE
        pltpu.make_async_remote_copy(
            mid.at[to], pair_got.at[z], row_send, row_recv, device_id=(aux, y * SIDE + to), device_id_type=MESH
        ).start()

    for k in FAR_FIRST[5:]:
        ship_column(k)

    own.wait()
    own_mid.wait()
    most = pl.ds(0, NAO - 1)
    pltpu.make_async_copy(part.at[seven], part.at[seven], col_send).wait()
    pltpu.make_async_copy(col_rows.at[seven], col_rows.at[seven], list_send).wait()
    pltpu.make_async_copy(mid.at[seven], mid.at[seven], row_send).wait()
    pltpu.make_async_copy(send.at[most], send.at[most], main_send).wait()
    pltpu.make_async_copy(pair_got.at[seven], pair_got.at[seven], row_recv).wait()
    pltpu.make_async_copy(got.at[most], got.at[most], main_recv).wait()


def exchange(rows, cols, tiles, coeff):
    vmem, hbm = pl.BlockSpec(memory_space=pltpu.VMEM), pl.BlockSpec(memory_space=pltpu.HBM)
    dma = pltpu.SemaphoreType.DMA
    bf16, f32 = jnp.bfloat16, jnp.float32
    return pl.pallas_call(
        exchange_kernel,
        out_shape=(
            jax.ShapeDtypeStruct((NAO, 3, 16, LANES), bf16),
            jax.ShapeDtypeStruct((SIDE, 8, LANES), f32),
        ),
        in_specs=[hbm, hbm, hbm, hbm],
        out_specs=(vmem, vmem),
        scratch_shapes=[
            pltpu.SMEM((1, NT), jnp.int32),
            pltpu.SMEM((1, NT), jnp.int32),
            pltpu.VMEM((OCC, NB * SB), bf16),
            pltpu.VMEM((NT, QD, SB * SB), bf16),
            pltpu.VMEM((2, SB * QD, LANES), f32),
            pltpu.VMEM((NAO, 3, 16, LANES), bf16),
            pltpu.VMEM((NT // 2, QD * OCC, LANES), bf16),
            pltpu.VMEM((3 * NB, OCC, LANES), bf16),
            pltpu.VMEM((2, OCC, NB * SB), bf16),
            pltpu.VMEM((QD, OCC, LANES), bf16),
            pltpu.VMEM((SIDE, OCC, LANES), bf16),
            pltpu.VMEM((SIDE, 8, LANES), f32),
            pltpu.VMEM((1, LANES), f32),
            pltpu.VMEM((SIDE, 1, LANES), f32),
            pltpu.SemaphoreType.REGULAR((SIDE,)), dma((3,)), dma((3,)), dma((2,)), dma((2,)), dma, dma, dma, dma, dma, dma, dma, dma, dma((4,)),
        ],
        compiler_params=pltpu.CompilerParams(collective_id=0, has_side_effects=True, vmem_limit_bytes=40 << 20),
        cost_estimate=pl.CostEstimate(flops=200_000_000, bytes_accessed=3_000_000, transcendentals=0),
        name="half_transform_exchange",
    )(rows, cols, tiles, coeff)


def place_kernel(got, pair_got, relaid, pair_ints, rows_vmem, rows, rows_sem, *sums):
    per = NAO // GROUPS
    low = lower_half((8, LANES))
    total, later = pair_got[0], pair_got[SIDE // 2]
    for k in range(1, SIDE // 2):
        total += pair_got[k]
        later += pair_got[SIDE // 2 + k]
    source = lax.broadcasted_iota(jnp.int32, (8, LANES), 1) // 16
    rows_vmem[...] = 8 * (jnp.where(low, swap_halves(total), later).astype(jnp.int32) + NB * source)
    fetch = pltpu.make_async_copy(rows_vmem, rows, rows_sem)
    fetch.start()
    pair_ints[...] = (total + later)[:, :OCC]
    for part in sums:
        part[...] = jnp.zeros(part.shape, jnp.float32)
    fetch.wait()

    @pl.loop(0, per)
    def _(k):
        for s in range(NT // 2):
            for g in range(GROUPS):
                v = got[g * per + k, s // 2, pl.ds(8 * (s % 2), 8), :].astype(jnp.float32)
                for side in range(2):
                    at = pl.ds(pl.multiple_of(rows[g, 16 * k + 2 * s + side], 8), 8)
                    sums[g][at, :] += jnp.where(low, v, 0.0) if side == 0 else jnp.where(low, 0.0, v)

    def block(b):
        g, local = divmod(b, per * NB)

        def at(i):
            return pl.ds(8 * i, 8)

        value = sums[g][at(local + NB), :]
        if local < NB and g > 0:
            value += sums[g - 1][at(local + (per + 1) * NB), :]
        if local >= (per - 1) * NB and g < GROUPS - 1:
            value += sums[g + 1][at(local - (per - 1) * NB), :]
        return value

    for tile in range(NAO * NB // 2):
        a, b = block(2 * tile), block(2 * tile + 1)
        value = jnp.where(low, a, b) + swap_halves(jnp.where(low, b, a))
        relaid[:, tile * LANES : (tile + 1) * LANES] = value.astype(jnp.bfloat16)


def place(got, pair_got):
    vmem = pl.BlockSpec(memory_space=pltpu.VMEM)
    per = NAO // GROUPS
    return pl.pallas_call(
        place_kernel,
        out_shape=(
            jax.ShapeDtypeStruct((8, NAO * NB * SB), jnp.bfloat16),
            jax.ShapeDtypeStruct((8, OCC), jnp.float32),
        ),
        in_specs=[vmem, vmem],
        out_specs=(vmem, vmem),
        scratch_shapes=[
            pltpu.VMEM((SIDE, LANES), jnp.int32),
            pltpu.SMEM((SIDE, LANES), jnp.int32),
            pltpu.SemaphoreType.DMA,
            *[pltpu.VMEM(((per + 2) * NB * 8, LANES), jnp.float32)] * GROUPS,
        ],
        compiler_params=pltpu.CompilerParams(vmem_limit_bytes=40 << 20),
        cost_estimate=pl.CostEstimate(flops=1_000_000, bytes_accessed=1_500_000, transcendentals=0),
        name="place",
    )(got, pair_got)


def per_device(tiles, slot_row_block, tile_col, coeff):
    operands = slot_row_block, tile_col, jnp.transpose(tiles, (1, 0, 2)), coeff.T
    got, pair_got = exchange(*(pltpu.with_memory_space_constraint(x, pltpu.HBM) for x in operands))
    return place(got, pair_got)


def solution(mesh):
    in_specs = (P("aux", "ao", None), P("aux", "ao"), P("aux", "ao"), P("ao", None))
    out_specs = (P(("aux", "ao"), None), P(("aux", "ao"), None))
    return jax.shard_map(per_device, mesh=mesh, in_specs=in_specs, out_specs=out_specs, check_vma=False)
```
